32 devices in a mesh: parts: 2 (over y), row: 2 (over x), col: 2 (over core), layer: 4 (over z).
Axes of the slice: x: 2, y: 2, z: 4, core: 2. Of those that a mesh axis runs over, the one named last changes fastest.
Arguments:
- dosages: bfloat16 [4096, 2048], P(('layer', 'col'), ('parts', 'row')), parts along dimension 1, may hold values from -6 to 6
- expression: bfloat16 [4096, 16384], P('layer', ('col', 'row')), may hold values from -6 to 6
Outputs:
- zscores: float32 [2048, 16384], P(('parts', 'row', 'layer'), 'col'), parts along dimension 0
The draws below stay inside these ranges and needn't reach their ends.
There are 2 independent parts, one for each index of `parts`. The reference program is written for one: setup_inputs(seed, part) draws one part's arguments, and reference() takes and returns one part's arrays. A program takes and returns all parts, laid end to end along the dimension named above; an argument that names none is the same for every part. Nothing has to cross between parts.
All inputs are finite; a program needn't handle non-finite values.
Results may differ from the reference program's by a relative error of at most 0.0003.
Values may be sent and summed in bfloat16 or wider, within the bound.
A program may use at most 128 MiB of HBM per device.

```python
import math
import jax
import jax.numpy as jnp

GENES = 16384
VARIANTS = 1024
SAMPLES = 4096


def level_of(rng, extent, shards, low, largest):
    level = 1.0
    for position, parts in shards:
        heights = jax.random.uniform(jax.random.fold_in(jax.random.fold_in(rng, 6), position), (parts,), jnp.float32, low / len(shards), largest / len(shards))
        level = level * jnp.repeat(jnp.exp(heights), extent[position] // parts).reshape((-1,) + (1,) * (len(extent) - 1 - position))
    return level


def scatter_about(rng, shape, scale, bound, shards=(), held_as=jnp.bfloat16):
    values = scale * jax.random.normal(rng, shape, jnp.float32)
    if shards:
        values = values * level_of(rng, shape, shards, -0.22, 0.18)
    return jnp.clip(values, -bound, bound).astype(held_as)


def setup_inputs(seed: int = 0, part: int = 0) -> dict:
    keys = jax.random.split(jax.random.key(seed), 3)
    part_keys = jax.random.split(jax.random.fold_in(keys[2], part), 3)
    return {
        "dosages": scatter_about(part_keys[0], (SAMPLES, VARIANTS), 1.0, 6.0, ((0, 8), (1, 2))),
        "expression": scatter_about(keys[1], (SAMPLES, GENES), 1.0, 6.0, ((0, 4), (1, 4))),
    }


def reference(dosages, expression):
    factor = 1.0 / math.sqrt(SAMPLES)
    cross = jnp.dot(dosages.T, expression, preferred_element_type=jnp.float32)
    return cross * factor
```

```python
import functools
import math

import jax
import jax.numpy as jnp
from jax import lax
from jax.experimental import pallas as pl
from jax.experimental.pallas import tpu as pltpu
from jax.sharding import PartitionSpec as P

OCTAVES = 22.0
TOP = 124.0
SLOPE = 2.0 * TOP / OCTAVES
MESH = pl.DeviceIdType.MESH
CHUNK = 256


def encoded(x, bound):
    exponent = SLOPE * (jnp.log2(jnp.abs(x)) - bound) + TOP
    code = jnp.exp2(jnp.clip(exponent, -TOP, TOP))
    return jnp.where(x < 0, -code, code).astype(jnp.bfloat16)


def decoded(code, bound):
    code = code.astype(jnp.float32)
    value = jnp.exp2((jnp.log2(jnp.abs(code)) - TOP) * (1.0 / SLOPE) + bound)
    return jnp.where(code < 0, -value, value)


def largest_square(ref, width):
    samples, columns = ref.shape
    rows = 64

    def over_columns(c, best):
        def over_rows(s, total):
            x = ref[pl.ds(pl.multiple_of(s * rows, rows), rows),
                    pl.ds(pl.multiple_of(c * width, width), width)].astype(jnp.float32)
            return total + jnp.sum((x * x).reshape(rows // 8, 8, width), axis=0)

        total = lax.fori_loop(0, samples // rows, over_rows, jnp.zeros((8, width), jnp.float32))
        return jnp.maximum(best, jnp.sum(total, axis=0, keepdims=True))

    best = lax.fori_loop(0, columns // width, over_columns, jnp.zeros((1, width), jnp.float32))
    return jnp.max(best, axis=1, keepdims=True)


def kernel(count, tiles, factor, d_ref, e_ref, out_ref,
           e_all, d_all, d_turned, part, far_out, far_in, near_out, near_in, both_out, both_in,
           result, bound_out, bound_in, e_square,
           e_sem, d_local, d_send, d_recv, d_core_send, d_core_recv,
           b_send, b_recv, far_send, far_recv, near_send, near_recv, both_send, both_recv,
           x_send, x_recv, x_local):
    row, col, layer = lax.axis_index("row"), lax.axis_index("col"), lax.axis_index("layer")
    up, down, far = (layer + 1) % 4, (layer + 3) % 4, (layer + 2) % 4
    mate = 1 - col
    items = count * tiles
    samples, variants = d_ref.shape
    width = e_all.shape[2]
    owned = variants // 4
    half = owned // 2
    chunks = width // CHUNK
    ways = ((0, up), (1, down))
    bound_ways = ways + ((2, far),)

    barrier = pltpu.get_barrier_semaphore()
    for to in (up, down, far):
        pl.semaphore_signal(barrier, inc=1, device_id={"layer": to}, device_id_type=MESH)
    pl.semaphore_signal(barrier, inc=1, device_id={"col": mate}, device_id_type=MESH)

    def greet(k, carry):
        pl.semaphore_signal(barrier, inc=1, device_id={"row": (row + k) % count}, device_id_type=MESH)
        return carry

    lax.fori_loop(1, count, greet, 0)

    def e_copy(t):
        return pltpu.make_async_copy(
            e_ref.at[:, pl.ds(pl.multiple_of(t * width, width), width)], e_all.at[t], e_sem.at[t])

    mine = pl.ds(pl.multiple_of(col * samples, samples), samples)
    own_d = pltpu.make_async_copy(d_ref, d_all.at[row, mine], d_local)
    own_d.start()
    for t in range(tiles):
        e_copy(t).start()

    pl.semaphore_wait(barrier, 3 + count)

    def core_copy(source, k):
        return pltpu.make_async_remote_copy(
            source, d_all.at[(row + count - k) % count, mine], d_core_send.at[k], d_core_recv.at[k],
            device_id={"col": mate}, device_id_type=MESH)

    def row_copy(k):
        return pltpu.make_async_remote_copy(
            d_ref, d_all.at[row, mine], d_send.at[k], d_recv.at[k],
            device_id={"row": (row + k) % count}, device_id_type=MESH)

    core_copy(d_ref, 0).start()
    lax.fori_loop(1, count, lambda k, carry: (row_copy(k).start(), carry)[1], 0)

    def bound_copy(which, way, to):
        return pltpu.make_async_remote_copy(
            bound_out.at[which], bound_in.at[which, way], b_send.at[which, way], b_recv.at[which, way],
            device_id={"layer": to}, device_id_type=MESH)

    def tell(which, d_square):
        square = jnp.maximum(d_square, 1e-30) * jnp.maximum(e_square[0:1, 0:1], 1e-30)
        bound_out[which] = jnp.broadcast_to(0.5 * jnp.log2(square) + 0.01, (8, CHUNK))
        for way, to in bound_ways:
            bound_copy(which, way, to).start()

    def turn(r):
        step = 256

        def body(s, carry):
            at = pl.ds(pl.multiple_of(s * step, step), step)
            d_turned[r, :, at] = d_all[r, at, :].T
            return carry

        lax.fori_loop(0, 2 * samples // step, body, 0)

    best = jnp.zeros((1, 1), jnp.float32)
    for t in range(tiles):
        e_copy(t).wait()
        best = jnp.maximum(best, largest_square(e_all.at[t], CHUNK))
    e_square[...] = jnp.broadcast_to(best, (8, 128))
    own_d.wait()
    core_copy(d_ref, 0).wait()
    tell(0, largest_square(d_all.at[row], CHUNK))
    turn(row)

    def place(i):
        j = (i + tiles - 1) % items
        return j // tiles, j % tiles

    def which_of(k):
        return (k + count - 1) // count

    def send(out, into, sends, recvs, i, way, to):
        return pltpu.make_async_remote_copy(
            out.at[i, way], into.at[i, way], sends.at[i, way], recvs.at[i, way],
            device_id={"layer": to}, device_id_type=MESH)

    far_copy = functools.partial(send, far_out, far_in, far_send, far_recv)
    near_copy = functools.partial(send, near_out, near_in, near_send, near_recv)
    both_copy = functools.partial(send, both_out, both_in, both_send, both_recv)

    def rows_of(owner, h):
        return pl.ds(pl.multiple_of(owner * owned + h * half, half), half)

    def over_chunks(body):
        def step(c, carry):
            body(pl.ds(pl.multiple_of(c * CHUNK, CHUNK), CHUNK))
            return carry

        lax.fori_loop(0, chunks, step, 0)

    def multiply(i):
        k, t = place(i)
        r = (row + k) % count
        slot = i % 3

        def body(at):
            part[slot, :, at] = jnp.dot(d_turned[r], e_all[t, :, at], preferred_element_type=jnp.float32)

        over_chunks(body)

    def first(i):
        k, _ = place(i)
        which, slot = which_of(k), i % 3

        for way, to in ways:
            def far_body(at):
                far_out[i, way, :, at] = encoded(part[slot, rows_of(far, way), at], bound_out[which, 0:1, :])

            over_chunks(far_body)
            far_copy(i, way, to).start()
        for way, to in ways:
            def near_body(at):
                near_out[i, way, :, at] = encoded(part[slot, rows_of(to, 1 - way), at], bound_out[which, 0:1, :])

            over_chunks(near_body)
            near_copy(i, way, to).start()

    def second(i):
        k, _ = place(i)
        which, slot = which_of(k), i % 3
        for way, to in ways:
            far_copy(i, way, to).wait_recv()

            def body(at):
                total = part[slot, rows_of(to, way), at] + decoded(
                    far_in[i, way, :, at], bound_in[which, way, 0:1, :])
                bound = jnp.maximum(bound_out[which, 0:1, :], bound_in[which, way, 0:1, :]) + 1.0
                both_out[i, way, :, at] = encoded(total, bound)

            over_chunks(body)
            both_copy(i, way, to).start()

    def local_out(i):
        _, t = place(i)
        at = pl.ds(pl.multiple_of((row * tiles + t) * width, width), width)
        return pltpu.make_async_copy(result.at[i], out_ref.at[:, at], x_local.at[i])

    def remote_out(i):
        k, t = place(i)
        at = pl.ds(pl.multiple_of((row * tiles + t) * width, width), width)
        return pltpu.make_async_remote_copy(
            result.at[i], out_ref.at[:, at], x_send.at[i], x_recv.at[i],
            device_id={"row": (row + k) % count}, device_id_type=MESH)

    def third(i):
        k, _ = place(i)
        which, slot = which_of(k), i % 3
        for way, to in ways:
            near_copy(i, way, to).wait_recv()
            both_copy(i, way, to).wait_recv()
        for h in range(2):
            def body(at):
                total = part[slot, rows_of(layer, h), at]
                bound = jnp.maximum(bound_in[which, h, 0:1, :], bound_in[which, 2, 0:1, :]) + 1.0
                total = total + decoded(both_in[i, h, :, at], bound)
                total = total + decoded(near_in[i, 1 - h, :, at], bound_in[which, 1 - h, 0:1, :])
                result[i, h * half:(h + 1) * half, at] = total * factor

            over_chunks(body)

        @pl.when(k == 0)
        def _():
            local_out(i).start()

        @pl.when(k != 0)
        def _():
            remote_out(i).start()

    def others():
        def take(k, best):
            row_copy(k).wait_recv()
            r = (row + count - k) % count
            core_copy(d_all.at[r, mine], k).start()
            return best

        lax.fori_loop(1, count, take, 0)

        def use(k, best):
            core_copy(d_ref, k).wait_recv()
            r = (row + count - k) % count
            turn(r)
            return jnp.maximum(best, largest_square(d_all.at[r], CHUNK))

        tell(1, lax.fori_loop(1, count, use, jnp.zeros((1, 1), jnp.float32)))

    def step(i, carry):
        @pl.when(i < items)
        def _():
            multiply(i)
            first(i)

        @pl.when(i == 0)
        def _():
            if count > 1:
                others()
            for way, to in bound_ways:
                bound_copy(0, way, to).wait_recv()

        @pl.when(i == 1)
        def _():
            if count > 1:
                for way, to in bound_ways:
                    bound_copy(1, way, to).wait_recv()

        @pl.when((i >= 1) & (i < items + 1))
        def _():
            second(i - 1)

        @pl.when(i >= 2)
        def _():
            third(i - 2)

        return carry

    lax.fori_loop(0, items + 2, step, 0)

    def finish(i, carry):
        k, _ = place(i)
        for way, to in ways:
            far_copy(i, way, to).wait_send()
            near_copy(i, way, to).wait_send()
            both_copy(i, way, to).wait_send()

        @pl.when(k == 0)
        def _():
            local_out(i).wait()

        @pl.when(k != 0)
        def _():
            remote_out(i).wait()

        return carry

    lax.fori_loop(0, items, finish, 0)
    for which in range(2 if count > 1 else 1):
        for way, to in bound_ways:
            bound_copy(which, way, to).wait_send()

    def finish_d(k, carry):
        row_copy(k).wait_send()
        core_copy(d_ref, k).wait_send()
        return carry

    lax.fori_loop(1, count, finish_d, 0)


def on_device(dosages, expression):
    count = lax.axis_size("row")
    assert lax.axis_size("layer") == 4 and lax.axis_size("col") == 2
    samples, variants = dosages.shape
    genes = expression.shape[1]
    width = min(1024, genes)
    tiles = genes // width
    items = count * tiles
    owned = variants // 4
    factor = 1.0 / math.sqrt(samples * 8)
    codes = pltpu.VMEM((items, 2, owned // 2, width), jnp.bfloat16)
    two = pltpu.SemaphoreType.DMA((items, 2))
    one = pltpu.SemaphoreType.DMA((items,))
    each = pltpu.SemaphoreType.DMA((count,))
    return pl.pallas_call(
        functools.partial(kernel, count, tiles, factor),
        out_shape=jax.ShapeDtypeStruct((owned, genes * count), jnp.float32),
        in_specs=[pl.BlockSpec(memory_space=pl.ANY)] * 2,
        out_specs=pl.BlockSpec(memory_space=pl.ANY),
        scratch_shapes=[
            pltpu.VMEM((tiles, 2 * samples, width), jnp.bfloat16),
            pltpu.VMEM((count, 2 * samples, variants), jnp.bfloat16),
            pltpu.VMEM((count, variants, 2 * samples), jnp.bfloat16),
            pltpu.VMEM((3, variants, width), jnp.float32),
            codes, codes, codes, codes, codes, codes,
            pltpu.VMEM((items, owned, width), jnp.float32),
            pltpu.VMEM((2, 8, CHUNK), jnp.float32),
            pltpu.VMEM((2, 3, 8, CHUNK), jnp.float32),
            pltpu.VMEM((8, 128), jnp.float32),
            pltpu.SemaphoreType.DMA((tiles,)), pltpu.SemaphoreType.DMA, each, each, each, each,
            pltpu.SemaphoreType.DMA((2, 3)), pltpu.SemaphoreType.DMA((2, 3)),
            two, two, two, two, two, two, one, one, one,
        ],
        compiler_params=pltpu.CompilerParams(
            collective_id=0, has_side_effects=True, vmem_limit_bytes=60 * 1024 * 1024),
        cost_estimate=pl.CostEstimate(
            flops=4 * samples * variants * genes * count, bytes_accessed=16 * 1024 * 1024, transcendentals=0),
    )(dosages, expression)


def solution(mesh):
    return jax.shard_map(
        on_device,
        mesh=mesh,
        in_specs=(P(("layer", "col"), ("parts", "row")), P("layer", ("col", "row"))),
        out_specs=P(("parts", "row", "layer"), "col"),
        check_vma=False,
    )
```

```python
import functools
import math

import jax
import jax.numpy as jnp
from jax import lax
from jax.experimental import pallas as pl
from jax.experimental.pallas import tpu as pltpu
from jax.sharding import PartitionSpec as P

OCTAVES = 22.0
TOP = 124.0
SLOPE = 2.0 * TOP / OCTAVES
MESH = pl.DeviceIdType.MESH
CHUNK = 256


def encoded(x, bound):
    exponent = SLOPE * (jnp.log2(jnp.abs(x)) - bound) + TOP
    code = jnp.exp2(jnp.clip(exponent, -TOP, TOP))
    return jnp.where(x < 0, -code, code).astype(jnp.bfloat16)


def decoded(code, bound):
    code = code.astype(jnp.float32)
    value = jnp.exp2((jnp.log2(jnp.abs(code)) - TOP) * (1.0 / SLOPE) + bound)
    return jnp.where(code < 0, -value, value)


def most(ref, rows, lanes):
    step = 64

    def over_rows(s, total):
        x = ref[pl.ds(pl.multiple_of(s * step, step), step), :].astype(jnp.float32)
        return total + jnp.sum((x * x).reshape(step // 8, 8, lanes), axis=0)

    total = lax.fori_loop(0, rows // step, over_rows, jnp.zeros((8, lanes), jnp.float32))
    return jnp.sum(total, axis=0, keepdims=True)


def kernel(count, tiles, factor, d_ref, e_ref, out_ref,
           e_near, e_far, d_all, part, kept, mid_out, mid_in, edge, result,
           square_out, square_in, bound_out, bound_in, rim_out, rim_in,
           e_sem, far_send, far_recv, y_send, y_recv, d_local, df_send, df_recv,
           row_send, row_recv, core_send, core_recv, mid_send, mid_recv, edge_send, edge_recv,
           x_send, x_recv, x_local, s_send, s_recv, b_send, b_recv, g_send, g_recv):
    parts, row = lax.axis_index("parts"), lax.axis_index("row")
    col, layer = lax.axis_index("col"), lax.axis_index("layer")
    inner = (layer + 1) % 4 // 2
    is_inner = (layer == 1) | (layer == 2)
    is_outer = (layer == 0) | (layer == 3)
    beside = layer // 2 * 2 + (1 - layer % 2)
    across = 3 - layer
    across_rim = 3 - beside
    mate = 1 - col
    variants, samples = d_ref.shape
    owned = variants // 4
    deep = 2 * samples

    barrier = pltpu.get_barrier_semaphore()

    def signal(where):
        pl.semaphore_signal(barrier, inc=1, device_id=where, device_id_type=MESH)

    signal({"layer": beside})
    signal({"layer": across})
    signal({"parts": 1 - parts})
    signal({"col": mate})
    lax.fori_loop(1, count, lambda k, c: (signal({"row": (row + k) % count}), c)[1], 0)

    def remote(source, target, send, recv, where):
        return pltpu.make_async_remote_copy(source, target, send, recv, device_id=where, device_id_type=MESH)

    def columns(start, size):
        return pl.ds(pl.multiple_of(start, 128), size)

    def e_copy(t):
        return pltpu.make_async_copy(e_ref.at[:, columns(t * CHUNK, CHUNK)], e_near.at[t], e_sem.at[t])

    def d_place(r, f):
        return d_all.at[r, :, columns((f * 2 + col) * samples, samples)]

    def d_far():
        return remote(d_ref, d_place(row, 1), df_send, df_recv, {"layer": beside})

    def d_row(k, f):
        return remote(d_place(row, f), d_place(row, f), row_send.at[f, k], row_recv.at[f, k],
                      {"row": (row + k) % count})

    def d_core(k, f):
        r = (row + count - k) % count
        return remote(d_place(r, f), d_place(r, f), core_send.at[f, k], core_recv.at[f, k], {"col": mate})

    def e_send(t):
        lanes = columns(parts * 128, 128)
        return remote(e_ref.at[:, columns(t * CHUNK + parts * 128, 128)], e_far.at[t, :, lanes],
                      far_send.at[t], far_recv.at[t], {"layer": beside})

    def y_copy(t):
        lanes = columns(parts * 128, 128)
        return remote(e_far.at[t, :, lanes], e_far.at[t, :, lanes], y_send.at[t], y_recv.at[t],
                      {"parts": 1 - parts})

    def square_copy():
        return remote(square_out, square_in, s_send, s_recv, {"layer": beside})

    def bound_copy():
        return remote(bound_out, bound_in, b_send, b_recv, {"layer": across})

    def rim_copy():
        return remote(rim_out, rim_in, g_send, g_recv, {"layer": beside})

    def mid_copy(t):
        return remote(mid_out.at[t], mid_in.at[t], mid_send.at[t], mid_recv.at[t], {"layer": across})

    def edge_copy(t):
        return remote(edge.at[t], edge.at[t], edge_send.at[t], edge_recv.at[t], {"layer": beside})

    def out_at(t):
        return out_ref.at[:, columns((row * tiles + t) * CHUNK, CHUNK)]

    def local_out(t):
        return pltpu.make_async_copy(result.at[t, 0], out_at(t), x_local.at[t])

    def remote_out(t, k):
        return remote(result.at[t, k], out_at(t), x_send.at[t, k], x_recv.at[t, k], {"row": (row + k) % count})

    own = pltpu.make_async_copy(d_ref, d_place(row, 0), d_local)
    own.start()
    lax.fori_loop(0, tiles, lambda t, c: (e_copy(t).start(), c)[1], 0)
    pl.semaphore_wait(barrier, 3 + count)

    @pl.when(is_outer)
    def _():
        d_far().start()
        d_far().wait_send()
        for t in range(min(2, tiles)):
            e_send(t).start()

    own.wait()
    d_core(0, 0).start()
    lax.fori_loop(1, count, lambda k, c: (d_row(k, 0).start(), c)[1], 0)

    def e_square(t, best):
        e_copy(t).wait()
        return jnp.maximum(best, most(e_near.at[t], deep, CHUNK))

    e_best = lax.fori_loop(0, tiles, e_square, jnp.zeros((1, CHUNK), jnp.float32))
    e_best = jnp.max(e_best, axis=1, keepdims=True)
    square_out[...] = jnp.broadcast_to(e_best, (8, CHUNK))

    def pass_on(f):
        def take(k, c):
            d_row(k, f).wait_recv()
            d_core(k, f).start()
            return c

        lax.fori_loop(1, count, take, 0)

    def arrived(f):
        lax.fori_loop(0, count, lambda k, c: (d_core(k, f).wait_recv(), c)[1], 0)

    def sent(f):
        lax.fori_loop(0, count, lambda k, c: (d_core(k, f).wait_send(), c)[1], 0)
        lax.fori_loop(1, count, lambda k, c: (d_row(k, f).wait_send(), c)[1], 0)

    def rows(r, owner):
        return d_all.at[r, pl.ds(pl.multiple_of(owner * owned, owned), owned), :]

    def finish(t, k, bound, codes):
        total = kept[t % 3, 0, k] + decoded(codes[...], bound)
        result[t, k] = total * factor

    def send_result(t):
        local_out(t).start()
        lax.fori_loop(1, count, lambda k, c: (remote_out(t, k).start(), c)[1], 0)

    def outer_program():
        square_copy().start()
        pass_on(0)
        arrived(0)

        def multiply(t):
            def body(k, c):
                left = rows((row + k) % count, layer)[:, pl.ds(0, deep)]
                kept[t % 3, 0, k] = jnp.dot(left, e_near[t], preferred_element_type=jnp.float32)
                return c

            lax.fori_loop(0, count, body, 0)

        def step(t, c):
            @pl.when(t + 2 < tiles)
            def _():
                e_send(t).wait_send()
                e_send(t + 2).start()

            @pl.when(t == LAG)
            def _():
                rim_copy().wait_recv()

            @pl.when(t >= LAG)
            def _():
                u = t - LAG
                multiply(u)
                edge_copy(u).wait_recv()
                lax.fori_loop(0, count, lambda k, c: (finish(u, k, rim_in[0:1, :], edge.at[u, k]), c)[1], 0)
                send_result(u)

            return c

        lax.fori_loop(0, tiles + LAG, step, 0)
        for t in range(max(tiles - 2, 0), tiles):
            e_send(t).wait_send()
        square_copy().wait_send()

    def inner_program():
        d_far().wait_recv()
        d_core(0, 1).start()
        lax.fori_loop(1, count, lambda k, c: (d_row(k, 1).start(), c)[1], 0)
        pass_on(0)
        e_send(0).wait_recv()
        y_copy(0).start()
        pass_on(1)
        if tiles > 1:
            e_send(1).wait_recv()
            y_copy(1).start()
        arrived(0)
        arrived(1)
        square_copy().wait_recv()

        def d_square(k, best):
            def body(s, best):
                x = d_all[k, pl.ds(pl.multiple_of(s * 16, 16), 16), :].astype(jnp.float32)
                return jnp.maximum(best, jnp.sum(x * x, axis=1, keepdims=True))

            return lax.fori_loop(0, variants // 16, body, best)

        d_best = lax.fori_loop(0, count, d_square, jnp.zeros((16, 1), jnp.float32))
        d_best = jnp.max(d_best, axis=0, keepdims=True)
        e_sum = square_out[...] + square_in[...]
        bound_out[...] = 0.5 * (jnp.log2(jnp.maximum(d_best, 1e-30)) + jnp.log2(jnp.maximum(e_sum, 1e-30))) + 0.01
        bound_copy().start()

        def multiply(t):
            def body(k, c):
                r = (row + k) % count
                part[...] = (
                    jnp.dot(d_all[r, :, 0:deep], e_near[t], preferred_element_type=jnp.float32))
                kept[t % 3, 1, k] = part[pl.ds(pl.multiple_of(beside * owned, owned), owned), :]
                part[...] += jnp.dot(d_all[r, :, deep:2 * deep], e_far[t], preferred_element_type=jnp.float32)
                kept[t % 3, 0, k] = part[pl.ds(pl.multiple_of(layer * owned, owned), owned), :]
                for n, owner in ((0, across), (1, across_rim)):
                    mid_out[t, n, k] = encoded(
                        part[pl.ds(pl.multiple_of(owner * owned, owned), owned), :], bound_out[0:1, :])
                return c

            lax.fori_loop(0, count, body, 0)
            mid_copy(t).start()

        def combine(t):
            mid_copy(t).wait_recv()

            def body(k, c):
                total = kept[t % 3, 1, k] + decoded(mid_in[t, 1, k], bound_in[0:1, :])
                edge[t, k] = encoded(total, rim_out[0:1, :])
                return c

            lax.fori_loop(0, count, body, 0)
            edge_copy(t).start()
            lax.fori_loop(0, count, lambda k, c: (finish(t, k, bound_in[0:1, :], mid_in.at[t, 0, k]), c)[1], 0)
            send_result(t)

        def step(t, c):
            @pl.when(t + 2 < tiles)
            def _():
                e_send(t + 2).wait_recv()
                y_copy(t + 2).start()

            @pl.when(t < tiles)
            def _():
                y_copy(t).wait_recv()
                multiply(t)

            @pl.when(t == 0)
            def _():
                bound_copy().wait_recv()
                rim_out[...] = jnp.maximum(bound_out[...], bound_in[...]) + 1.0
                rim_copy().start()

            @pl.when(t >= 1)
            def _():
                combine(t - 1)

            return c

        lax.fori_loop(0, tiles + 1, step, 0)

        def done(t, c):
            y_copy(t).wait_send()
            mid_copy(t).wait_send()
            edge_copy(t).wait_send()
            return c

        lax.fori_loop(0, tiles, done, 0)
        bound_copy().wait_send()
        rim_copy().wait_send()
        sent(1)

    pl.when(is_outer)(outer_program)
    pl.when(is_inner)(inner_program)
    sent(0)

    def last(t, c):
        local_out(t).wait()
        return lax.fori_loop(1, count, lambda k, c: (remote_out(t, k).wait(), c)[1], c)

    lax.fori_loop(0, tiles, last, 0)


LAG = 8


def on_device(dosages, expression):
    count = lax.axis_size("row")
    assert lax.axis_size("layer") == 4 and lax.axis_size("col") == 2 and lax.axis_size("parts") == 2
    samples, variants = dosages.shape
    genes = expression.shape[1]
    tiles = genes // CHUNK
    owned = variants // 4
    factor = 1.0 / math.sqrt(samples * 8)
    dma = pltpu.SemaphoreType.DMA
    note = pltpu.VMEM((8, CHUNK), jnp.float32)
    tile = pltpu.VMEM((tiles, 2 * samples, CHUNK), jnp.bfloat16)
    mid = pltpu.VMEM((tiles, 2, count, owned, CHUNK), jnp.bfloat16)
    per_tile, per_row, per_out = dma((tiles,)), dma((2, count)), dma((tiles, count))
    return pl.pallas_call(
        functools.partial(kernel, count, tiles, factor),
        out_shape=jax.ShapeDtypeStruct((owned, genes * count), jnp.float32),
        in_specs=[pl.BlockSpec(memory_space=pl.ANY)] * 2,
        out_specs=pl.BlockSpec(memory_space=pl.ANY),
        scratch_shapes=[
            tile, tile,
            pltpu.VMEM((count, variants, 4 * samples), jnp.bfloat16),
            pltpu.VMEM((variants, CHUNK), jnp.float32),
            pltpu.VMEM((3, 2, count, owned, CHUNK), jnp.float32),
            mid, mid,
            pltpu.VMEM((tiles, count, owned, CHUNK), jnp.bfloat16),
            pltpu.VMEM((tiles, count, owned, CHUNK), jnp.float32),
            note, note, note, note, note, note,
            per_tile, per_tile, per_tile, per_tile, per_tile, dma, dma, dma,
            per_row, per_row, per_row, per_row, per_tile, per_tile, per_tile, per_tile,
            per_out, per_out, per_tile, dma, dma, dma, dma, dma, dma,
        ],
        compiler_params=pltpu.CompilerParams(
            collective_id=0, has_side_effects=True, vmem_limit_bytes=62 * 1024 * 1024),
        cost_estimate=pl.CostEstimate(
            flops=8 * samples * variants * genes * count, bytes_accessed=16 * 1024 * 1024, transcendentals=0),
    )(dosages.T, expression)


def solution(mesh):
    return jax.shard_map(
        on_device,
        mesh=mesh,
        in_specs=(P(("layer", "col"), ("parts", "row")), P("layer", ("col", "row"))),
        out_specs=P(("parts", "row", "layer"), "col"),
        check_vma=False,
    )
```
